32 devices in a mesh: ctx: 16 (over z, y, core), kvh: 2 (over x).
Axes of the slice: x: 2, y: 2, z: 4, core: 2. Of those that a mesh axis runs over, the one named last changes fastest.
Arguments:
- queries: bfloat16 [2048, 2048], P(('ctx', 'kvh')), may hold values from -180 to 180
- keys: bfloat16 [2048, 256], P(('ctx', 'kvh')), may hold values from -6 to 6
- values: bfloat16 [2048, 256], P(('ctx', 'kvh')), may hold values from -6 to 6
Outputs:
- attended: bfloat16 [2048, 2048], P(('ctx', 'kvh'))
The draws below stay inside these ranges and needn't reach their ends.
All inputs are finite; a program needn't handle non-finite values.
Results may differ from the reference program's by a relative error of at most 0.006.
Values may be sent and summed in bfloat16 or wider, within the bound.
No kernel may reach another device: no remote copies, remote signals or barrier semaphores. Data moves between devices by JAX's collectives and lax.ppermute only.
A program may use at most 64 MiB of HBM per device.

```python
import math
import jax
import jax.numpy as jnp
from jax import lax

HD = 128
QPG = 8
KVH = 2
TOKENS = 2048


def shared_keys(key):
    basis = jnp.clip(jax.random.normal(key, (TOKENS, KVH * HD), jnp.float32), -6.0, 6.0)
    return basis


def draw_keys(key, part):
    basis = shared_keys(key)
    return basis.astype(jnp.bfloat16)


def draw_queries(key, part):
    key = jax.random.fold_in(key, 5)
    drawn = jnp.clip(jax.random.normal(key, (TOKENS, KVH, QPG, HD), jnp.float32), -6.0, 6.0)
    return drawn.reshape(TOKENS, KVH * QPG * HD).astype(jnp.bfloat16)


def levels(stream_key, dims, shards, least, top_value):
    gain = 1.0
    for axis_at, blocks in shards:
        heights = jax.random.uniform(jax.random.fold_in(jax.random.fold_in(stream_key, 6), axis_at), (blocks,), jnp.float32, least / len(shards), top_value / len(shards))
        gain = gain * jnp.repeat(jnp.exp(heights), dims[axis_at] // blocks).reshape((-1,) + (1,) * (len(dims) - 1 - axis_at))
    return gain


def bell_draw(stream_key, dims, scale, limit, split=(), kind=jnp.bfloat16):
    drawn = scale * jax.random.normal(stream_key, dims, jnp.float32)
    if split:
        drawn = drawn * levels(stream_key, dims, split, -0.22, 0.18)
    return jnp.clip(drawn, -limit, limit).astype(kind)


def setup_inputs(seed: int = 0) -> dict:
    seeds = jax.random.split(jax.random.key(seed), 4)
    queries = draw_queries(jax.random.fold_in(seeds[3], 71), 0)
    keys = draw_keys(jax.random.fold_in(seeds[3], 71), 0)
    values = bell_draw(seeds[2], (TOKENS, KVH * HD), 1.0, 6.0, ((0, 32),))
    return {"queries": queries, "keys": keys, "values": values}


def reference(queries, keys, values):
    total = queries.shape[0]
    factor = 1.0 / math.sqrt(HD)
    query_heads = queries.reshape(total, KVH, QPG, HD).astype(jnp.float32)
    key_heads = keys.reshape(total, KVH, HD).astype(jnp.float32)
    value_heads = values.reshape(total, KVH, HD).astype(jnp.float32)
    width = min(512, total)
    outputs = []
    for first in range(0, total, width):
        final = first + width
        query_group = jnp.transpose(query_heads[first:final], (1, 0, 2, 3))
        key_group = jnp.transpose(key_heads[:final], (1, 0, 2))
        value_group = jnp.transpose(value_heads[:final], (1, 0, 2))
        query_place = jnp.arange(first, final, dtype=jnp.int32)
        key_place = jnp.arange(0, final, dtype=jnp.int32)
        visible = key_place[None, :] <= query_place[:, None]

        def one_group(operands):
            group_query, group_key, group_value = operands
            scores = jnp.einsum('bhd,kd->hbk', group_query, group_key) * factor
            scores = jnp.where(visible[None], scores, -1e+30)
            largest = lax.optimization_barrier(jnp.max(scores, axis=-1, keepdims=True))
            weights = jnp.where(visible[None], jnp.exp(scores - largest), 0.0)
            totals = lax.optimization_barrier(jnp.sum(weights, axis=-1))
            rounded = lax.optimization_barrier(weights.astype(jnp.bfloat16)).astype(jnp.float32)
            mixed = jnp.einsum('hbk,kd->bhd', rounded, group_value)
            return mixed / jnp.transpose(totals)[:, :, None]
        results = lax.map(one_group, (query_group, key_group, value_group))
        outputs.append(jnp.transpose(results, (1, 0, 2, 3)).reshape(width, KVH * QPG * HD))
    return jnp.concatenate(outputs, axis=0).astype(jnp.bfloat16)
```

```python
import functools
import math

import jax
import jax.numpy as jnp
from jax import lax
from jax.experimental import pallas as pl
from jax.experimental.pallas import tpu as pltpu
from jax.sharding import PartitionSpec as P

HD = 128
AXES = ("ctx", "kvh")
CORES = 2
HIDDEN = -1e30


class Layout:
    def __init__(self, mesh_shape):
        ctx, self.across = mesh_shape["ctx"], mesh_shape["kvh"]
        self.lines = 2
        self.planes = ctx // (CORES * self.lines)
        self.size = ctx * self.across
        self.mixed = self.lines == self.across

    def split(self, rank):
        column = rank % self.across
        core = rank // self.across % CORES
        line = rank // (self.across * CORES) % self.lines
        plane = rank // (self.across * CORES * self.lines)
        return plane, line, core, column

    def join(self, plane, line, core, column):
        return ((plane * self.lines + line) * CORES + core) * self.across + column

    def moved(self, place, first, second):
        plane, line, core, column = place
        if self.mixed:
            by_line = jnp.where(core == 0, second, first) if not isinstance(core, int) else (first if core else second)
            by_column = first + second - by_line
        else:
            by_line, by_column = second, first
        return plane, (line + by_line) % self.lines, core, (column + by_column) % self.across

    def firsts(self):
        return self.across

    def seconds(self):
        return self.lines

    def pairs(self, move):
        found = []
        for rank in range(self.size):
            target = move(self.split(rank))
            if target is not None:
                found.append((rank, self.join(*target)))
        return found


def gather_pieces(layout, block):
    def up(steps):
        def move(place):
            plane, line, core, column = place
            return (plane + steps, line, core, column) if plane + steps < layout.planes else None

        return layout.pairs(move)

    def on(first, second):
        return layout.pairs(lambda place: layout.moved(place, first, second))

    other = layout.pairs(lambda place: (place[0], place[1], 1 - place[2], place[3]))
    column = [block] + [lax.ppermute(block, AXES, up(steps)) for steps in range(1, layout.planes)]
    column = jnp.concatenate(column, axis=0)
    held = {(0, 0): column}
    for first in range(1, layout.firsts()):
        held[first, 0] = lax.ppermute(column, AXES, on(first, 0))
    for second in range(1, layout.seconds()):
        held[0, second] = lax.ppermute(column, AXES, on(0, second))
    for first in range(1, layout.firsts()):
        for second in range(1, layout.seconds()):
            held[first, second] = lax.ppermute(held[first, 0], AXES, on(0, second))
    places = sorted(held)
    own = [held[place] for place in places]
    swapped = [lax.ppermute(piece, AXES, other) for piece in own]
    return places, own + swapped


def attend_kernel(layout, places, rows, *refs):
    query_ref, refs = refs[0], refs[1:]
    count = 2 * len(places)
    key_refs, value_refs, out_ref, score_ref = refs[:count], refs[count : 2 * count], refs[-2], refs[-1]
    rank = lax.axis_index("ctx") * layout.across + lax.axis_index("kvh")
    plane, line, core, column = layout.split(rank)
    heads = query_ref.shape[1] // HD
    width = key_refs[0].shape[0]
    query = jnp.concatenate([query_ref[:, h * HD : (h + 1) * HD] for h in range(heads)], axis=0)
    along = lax.broadcasted_iota(jnp.int32, (1, width), 1)
    for at in range(count):
        first, second = places[at % len(places)]
        own_core = at < len(places)
        there = core if own_core else 1 - core
        _, source_line, _, source_column = layout.moved((plane, line, there, column), -first, -second)
        bias = jnp.zeros((1, width), jnp.float32)
        for steps in range(layout.planes):
            source = layout.join(plane - steps, source_line, there, source_column)
            hidden = jnp.logical_or(plane < steps, source > rank)
            level = jnp.where(hidden, jnp.float32(HIDDEN), jnp.float32(0.0))
            bias = jnp.where(along // rows == steps, level, bias)
        scores = lax.dot_general(
            query, key_refs[at][...], (((1,), (1,)), ((), ())), preferred_element_type=jnp.float32
        )
        scores = scores + bias
        if at == 0:
            token = lax.broadcasted_iota(jnp.int32, scores.shape, 0) % rows
            place = lax.broadcasted_iota(jnp.int32, scores.shape, 1)
            scores = jnp.where(jnp.logical_and(place < rows, place > token), HIDDEN, scores)
        score_ref[:, at * width : (at + 1) * width] = scores
    scale = math.log2(math.e) / math.sqrt(HD)
    largest = jnp.max(score_ref[...], axis=1, keepdims=True) * scale
    totals = jnp.zeros((heads * rows, 1), jnp.float32)
    summed = jnp.zeros((heads * rows, HD), jnp.float32)
    for at in range(count):
        weights = jnp.exp2(score_ref[:, at * width : (at + 1) * width] * scale - largest)
        totals = totals + jnp.sum(weights, axis=1, keepdims=True)
        summed = summed + jnp.dot(
            weights.astype(jnp.bfloat16), value_refs[at][...], preferred_element_type=jnp.float32
        )
    result = (summed / totals).astype(jnp.bfloat16)
    for h in range(heads):
        out_ref[:, h * HD : (h + 1) * HD] = result[h * rows : (h + 1) * rows]


def attend(layout, places, queries, pieces, groups):
    rows, query_width = queries.shape
    width = pieces[0].shape[0]
    per_group = query_width // groups

    def spec(offset):
        return pl.BlockSpec((width, HD), lambda g: (0, offset + g))

    tokens = width * len(pieces)
    return pl.pallas_call(
        functools.partial(attend_kernel, layout, places, rows),
        grid=(groups,),
        in_specs=[pl.BlockSpec((rows, per_group), lambda g: (0, g))]
        + [spec(0) for _ in pieces]
        + [spec(groups) for _ in pieces],
        out_specs=pl.BlockSpec((rows, per_group), lambda g: (0, g)),
        out_shape=jax.ShapeDtypeStruct((rows, query_width), jnp.bfloat16),
        scratch_shapes=[pltpu.VMEM((rows * per_group // HD, tokens), jnp.float32)],
        compiler_params=pltpu.CompilerParams(vmem_limit_bytes=32 * 1024 * 1024),
        cost_estimate=pl.CostEstimate(
            flops=4 * rows * query_width * tokens, bytes_accessed=4 * tokens * groups * HD, transcendentals=0
        ),
    )(queries, *pieces, *pieces)


def solution(mesh):
    layout = Layout(dict(mesh.shape))

    def per_device(queries, keys, values):
        block = jnp.concatenate([keys, values], axis=1)
        places, pieces = gather_pieces(layout, block)
        return attend(layout, places, queries, pieces, keys.shape[1] // HD)

    placed = P(AXES, None)
    return jax.shard_map(
        per_device, mesh=mesh, in_specs=(placed, placed, placed), out_specs=placed, check_vma=False
    )
```

```python
import functools
import math

import jax
import jax.numpy as jnp
from jax import lax
from jax.experimental import pallas as pl
from jax.experimental.pallas import tpu as pltpu
from jax.sharding import PartitionSpec as P

HD = 128
AXES = ("ctx", "kvh")
CORES = 2
HIDDEN = -1e30


class Layout:
    def __init__(self, mesh_shape):
        ctx, self.across = mesh_shape["ctx"], mesh_shape["kvh"]
        self.lines = 2
        self.planes = ctx // (CORES * self.lines)
        self.size = ctx * self.across
        self.mixed = self.lines == self.across

    def split(self, rank):
        column = rank % self.across
        core = rank // self.across % CORES
        line = rank // (self.across * CORES) % self.lines
        plane = rank // (self.across * CORES * self.lines)
        return plane, line, core, column

    def join(self, plane, line, core, column):
        return ((plane * self.lines + line) * CORES + core) * self.across + column

    def partner(self, place, up=0, first=0, second=0, swap=0):
        plane, line, core, column = place
        if self.mixed:
            by_line = core * first + (1 - core) * second
            by_column = core * second + (1 - core) * first
        else:
            by_line, by_column = second, first
        return plane ^ up, line ^ by_line, core ^ swap, column ^ by_column

    def exchange(self, array, **steps):
        pairs = [(rank, self.join(*self.partner(self.split(rank), **steps))) for rank in range(self.size)]
        return lax.ppermute(array, AXES, pairs)

    def here(self):
        return lax.axis_index("ctx") * self.across + lax.axis_index("kvh")


def fold_kernel(layout, sources, rows, carried, last, *refs):
    refs = list(refs)
    query_ref = refs.pop(0)
    state_refs = [refs.pop(0) for _ in range(2)] if carried else None
    count = len(sources)
    key_refs, value_refs = refs[:count], refs[count : 2 * count]
    out_refs, score_ref = refs[2 * count : -1], refs[-1]
    rank = layout.here()
    place = layout.split(rank)
    heads = query_ref.shape[1] // HD
    query = jnp.concatenate([query_ref[:, h * HD : (h + 1) * HD] for h in range(heads)], axis=0)
    begin = 0
    spans = []
    for blocks, key_ref in zip(sources, key_refs, strict=True):
        width = key_ref.shape[0]
        along = lax.broadcasted_iota(jnp.int32, (1, width), 1)
        bias = jnp.zeros((1, width), jnp.float32)
        scores = lax.dot_general(
            query, key_ref[...], (((1,), (1,)), ((), ())), preferred_element_type=jnp.float32
        )
        for at, (up, first, second, swap) in enumerate(blocks):
            plane, line, core, column = place
            there = layout.partner((plane, line, core ^ swap, column), up=up, first=first, second=second)
            source = layout.join(*there)
            level = jnp.where(source > rank, jnp.float32(HIDDEN), jnp.float32(0.0))
            bias = jnp.where(along // rows == at, level, bias)
        scores = scores + bias
        for at, steps in enumerate(blocks):
            if steps == (0, 0, 0, 0):
                token = lax.broadcasted_iota(jnp.int32, scores.shape, 0) % rows
                key_at = lax.broadcasted_iota(jnp.int32, scores.shape, 1) - at * rows
                later = jnp.logical_and(key_at < rows, key_at > token)
                scores = jnp.where(jnp.logical_and(key_at >= 0, later), HIDDEN, scores)
        score_ref[:, begin : begin + width] = scores
        spans.append((begin, begin + width))
        begin += width
    scale = math.log2(math.e) / math.sqrt(HD)
    largest = jnp.max(score_ref[...], axis=1, keepdims=True) * scale
    if carried:
        summed_ref, stat_ref = state_refs
        largest_old = stat_ref[0, :, 0:1]
        largest = jnp.maximum(largest, largest_old)
        decay = jnp.exp2(largest_old - largest)
        totals = stat_ref[0, :, 1:2] * decay
        summed = summed_ref[0] * decay
    else:
        totals = jnp.zeros((heads * rows, 1), jnp.float32)
        summed = jnp.zeros((heads * rows, HD), jnp.float32)
    for (start, end), value_ref in zip(spans, value_refs, strict=True):
        weights = jnp.exp2(score_ref[:, start:end] * scale - largest)
        totals = totals + jnp.sum(weights, axis=1, keepdims=True)
        summed = summed + jnp.dot(
            weights.astype(jnp.bfloat16), value_ref[...], preferred_element_type=jnp.float32
        )
    if last:
        result = (summed / totals).astype(jnp.bfloat16)
        for h in range(heads):
            out_refs[0][:, h * HD : (h + 1) * HD] = result[h * rows : (h + 1) * rows]
    else:
        out_refs[0][0] = summed
        lane = lax.broadcasted_iota(jnp.int32, (heads * rows, HD), 1)
        out_refs[1][0] = jnp.where(lane == 0, largest, totals)


def fold(layout, queries, state, pieces, groups, last=False):
    rows, query_width = queries.shape
    per_group = query_width // groups
    tall = rows * per_group // HD
    arrays = [array for array, _ in pieces]
    tokens = sum(array.shape[0] for array in arrays)

    def spec(array, offset):
        return pl.BlockSpec((array.shape[0], HD), lambda g: (0, offset + g))

    row_spec = pl.BlockSpec((rows, per_group), lambda g: (0, g))
    state_spec = pl.BlockSpec((1, tall, HD), lambda g: (g, 0, 0))
    state_type = jax.ShapeDtypeStruct((groups, tall, HD), jnp.float32)
    carried = state is not None
    return pl.pallas_call(
        functools.partial(fold_kernel, layout, [blocks for _, blocks in pieces], rows, carried, last),
        grid=(groups,),
        in_specs=[row_spec]
        + [state_spec] * (2 if carried else 0)
        + [spec(array, 0) for array in arrays]
        + [spec(array, groups) for array in arrays],
        out_specs=row_spec if last else [state_spec] * 2,
        out_shape=jax.ShapeDtypeStruct(queries.shape, jnp.bfloat16) if last else [state_type] * 2,
        scratch_shapes=[pltpu.VMEM((tall, tokens), jnp.float32)],
        compiler_params=pltpu.CompilerParams(vmem_limit_bytes=32 * 1024 * 1024),
        cost_estimate=pl.CostEstimate(flops=0, bytes_accessed=0, transcendentals=0),
    )(queries, *(state or ()), *arrays, *arrays)


def solution(mesh):
    layout = Layout(dict(mesh.shape))

    def per_device(queries, keys, values):
        groups = keys.shape[1] // HD
        exchange = layout.exchange
        block = jnp.concatenate([keys, values], axis=1)
        ups = range(1, layout.planes)
        firsts = range(1, layout.lines if layout.mixed else layout.across)
        seconds = range(1, layout.lines)
        above_steps = [(up, 0, 0) for up in reversed(ups)]
        flat_steps = [(0, f, 0) for f in firsts] + [(0, 0, s) for s in seconds]
        flat_steps += [(0, f, s) for f in firsts for s in seconds]
        above, flat = lax.optimization_barrier(
            (
                [exchange(block, up=up) for up, _, _ in above_steps],
                [exchange(block, first=f, second=s) for _, f, s in flat_steps],
            )
        )
        above = jnp.concatenate(above, axis=0)
        flat_steps = [(0, 0, 0)] + flat_steps
        flat = jnp.concatenate([block] + flat, axis=0)

        def both(array, steps):
            return [
                (array, [(*at, 0) for at in steps]),
                (exchange(array, swap=1), [(*at, 1) for at in steps]),
            ]

        def shifted(f, s):
            return [(up, f, s) for up, _, _ in above_steps]

        by_first = {f: exchange(above, first=f) for f in firsts}
        by_second = {s: exchange(above, second=s) for s in seconds}
        state = fold(layout, queries, None, both(flat, flat_steps), groups)
        state = fold(layout, queries, state, both(above, above_steps), groups)
        by_first, state = lax.optimization_barrier((by_first, state))
        by_second, state = lax.optimization_barrier((by_second, state))
        corners = {(f, s): exchange(by_first[f], second=s) for f in firsts for s in seconds}
        sides = []
        for f in firsts:
            sides += both(by_first[f], shifted(f, 0))
        for s in seconds:
            sides += both(by_second[s], shifted(0, s))
        state = fold(layout, queries, state, sides, groups)
        corners, state = lax.optimization_barrier((corners, state))
        ends = []
        for (f, s), array in corners.items():
            ends += both(array, shifted(f, s))
        return fold(layout, queries, state, ends, groups, last=True)

    placed = P(AXES, None)
    return jax.shard_map(
        per_device, mesh=mesh, in_specs=(placed, placed, placed), out_specs=placed, check_vma=False
    )
```

```python
import functools
import math

import jax
import jax.numpy as jnp
from jax import lax
from jax.experimental import pallas as pl
from jax.experimental.pallas import tpu as pltpu
from jax.sharding import PartitionSpec as P

HD = 128
AXES = ("ctx", "kvh")
CORES = 2
HIDDEN = -1e30


class Layout:
    def __init__(self, mesh_shape):
        ctx, self.across = mesh_shape["ctx"], mesh_shape["kvh"]
        self.lines = 2
        self.planes = ctx // (CORES * self.lines)
        self.size = ctx * self.across

    def split(self, rank):
        column = rank % self.across
        core = rank // self.across % CORES
        line = rank // (self.across * CORES) % self.lines
        plane = rank // (self.across * CORES * self.lines)
        return plane, line, core, column

    def join(self, plane, line, core, column):
        return ((plane * self.lines + line) * CORES + core) * self.across + column

    def partner(self, rank, up=0, line=0, swap=0, column=0):
        place = self.split(rank)
        return self.join(place[0] ^ up, place[1] ^ line, place[2] ^ swap, place[3] ^ column)

    def exchange(self, array, **steps):
        return lax.ppermute(array, AXES, [(rank, self.partner(rank, **steps)) for rank in range(self.size)])

    def here(self):
        return lax.axis_index("ctx") * self.across + lax.axis_index("kvh")


def fold_kernel(layout, sources, rows, groups, carried, last, *refs):
    refs = list(refs)
    query_ref = refs.pop(0)
    state_refs = [refs.pop(0) for _ in range(3)] if carried else None
    piece_refs, refs = refs[: len(sources)], refs[len(sources) :]
    out_refs, (score_ref, weight_ref) = refs[:-2], refs[-2:]
    blocks = [steps for piece in sources for steps in piece]
    width = len(blocks) * rows
    heads = query_ref.shape[1] // (groups * HD)
    tall = heads * rows
    scale = math.log2(math.e) / math.sqrt(HD)

    rank = layout.here()
    along = lax.broadcasted_iota(jnp.int32, (1, width), 1)
    bias = jnp.zeros((1, width), jnp.float32)
    for at, (up, line, swap, column) in enumerate(blocks):
        hidden = layout.partner(rank, up, line, swap, column) > rank
        bias = jnp.where(along // rows == at, jnp.where(hidden, HIDDEN, 0.0).astype(jnp.float32), bias)
    own = blocks.index((0, 0, 0, 0)) * rows if (0, 0, 0, 0) in blocks else None
    if own is not None:
        token = lax.broadcasted_iota(jnp.int32, (rows, width), 0)
        place = lax.broadcasted_iota(jnp.int32, (rows, width), 1) - own
        later = jnp.logical_and(place < rows, place > token)
        bias = jnp.where(jnp.logical_and(place >= 0, later), HIDDEN, bias)

    for group in range(groups):
        first = group * heads * HD
        query = jnp.concatenate([query_ref[:, first + h * HD : first + (h + 1) * HD] for h in range(heads)], axis=0)
        at = group * HD
        key = jnp.concatenate([ref[:, at : at + HD] for ref in piece_refs], axis=0)
        at = (groups + group) * HD
        value = jnp.concatenate([ref[:, at : at + HD] for ref in piece_refs], axis=0)
        score_ref[...] = lax.dot_general(
            query, key, (((1,), (1,)), ((), ())), preferred_element_type=jnp.float32
        )
        tops, sums = [], []
        for begin in range(0, tall, rows):
            scores = score_ref[begin : begin + rows, :] * scale + bias
            top = jnp.broadcast_to(jnp.max(scores, axis=1, keepdims=True), (rows, HD))
            if carried:
                top = jnp.maximum(top, state_refs[0][group, begin : begin + rows])
            total = jnp.zeros((rows, HD), jnp.float32)
            rest = jnp.zeros((rows, 1), jnp.float32)
            for left in range(0, width, HD):
                part = min(HD, width - left)
                weights = jnp.exp2(scores[:, left : left + part] - top[:, :part])
                if part == HD:
                    total = total + weights
                else:
                    rest = jnp.sum(weights, axis=1, keepdims=True)
                weight_ref[begin : begin + rows, left : left + part] = weights.astype(jnp.bfloat16)
            tops.append(top)
            sums.append(jnp.broadcast_to(jnp.sum(total, axis=1, keepdims=True) + rest, (rows, HD)))
        largest, totals = jnp.concatenate(tops, axis=0), jnp.concatenate(sums, axis=0)
        summed = jnp.dot(weight_ref[...], value, preferred_element_type=jnp.float32)
        if carried:
            decay = jnp.exp2(state_refs[0][group] - largest)
            totals = totals + state_refs[1][group] * decay
            summed = summed + state_refs[2][group] * decay
        if last:
            result = (summed / totals).astype(jnp.bfloat16)
            for h in range(heads):
                out_refs[0][:, first + h * HD : first + (h + 1) * HD] = result[h * rows : (h + 1) * rows]
        else:
            for ref, array in zip(out_refs, (largest, totals, summed), strict=True):
                ref[group] = array


def fold(layout, queries, state, pieces, groups, last=False):
    rows, query_width = queries.shape
    tall = rows * query_width // (groups * HD)
    arrays = [array for array, _ in pieces]
    tokens = sum(array.shape[0] for array in arrays)
    carried = state is not None
    state_type = jax.ShapeDtypeStruct((groups, tall, HD), jnp.float32)
    whole = pl.BlockSpec(memory_space=pltpu.VMEM)
    return pl.pallas_call(
        functools.partial(
            fold_kernel, layout, [blocks for _, blocks in pieces], rows, groups, carried, last
        ),
        in_specs=[whole] * (1 + 3 * carried + len(arrays)),
        out_specs=whole if last else [whole] * 3,
        out_shape=jax.ShapeDtypeStruct(queries.shape, jnp.bfloat16) if last else [state_type] * 3,
        scratch_shapes=[pltpu.VMEM((tall, tokens), jnp.float32), pltpu.VMEM((tall, tokens), jnp.bfloat16)],
        compiler_params=pltpu.CompilerParams(vmem_limit_bytes=24 * 1024 * 1024),
        cost_estimate=pl.CostEstimate(flops=0, bytes_accessed=0, transcendentals=0),
    )(queries, *(state or ()), *arrays)


def solution(mesh):
    layout = Layout(dict(mesh.shape))

    def per_device(queries, keys, values):
        groups = keys.shape[1] // HD
        exchange = layout.exchange
        block = jnp.concatenate([keys, values], axis=1)
        ups = range(1, layout.planes)
        lines = range(1, layout.lines)
        columns = range(1, layout.across)
        corners = [(0, l, 0, c) for l in lines for c in columns]

        def go(array, steps):
            return exchange(array, up=steps[0], line=steps[1], swap=steps[2], column=steps[3])

        def join(arrays):
            return jnp.concatenate(arrays, axis=0) if len(arrays) > 1 else arrays[0]

        def moved(steps, by):
            return [tuple(a ^ b for a, b in zip(one, by, strict=True)) for one in steps]

        def swapped(pieces):
            return [(exchange(array, swap=1), moved(steps, (0, 0, 1, 0))) for array, steps in pieces]

        corner = join([go(block, steps) for steps in corners])
        above_steps = [(up, 0, 0, 0) for up in reversed(ups)]
        above = join([go(block, steps) for steps in above_steps])
        side_steps = [(0, l, 0, 0) for l in lines] + [(0, 0, 0, c) for c in columns]
        flat = join([block] + [go(block, steps) for steps in side_steps] + [corner])
        flat_steps = [(0, 0, 0, 0)] + side_steps + corners
        far = [go(corner, steps) for steps in above_steps]
        sides = [go(above, steps) for steps in side_steps]

        near = [(flat, flat_steps), (above, above_steps)]
        state = fold(layout, queries, None, near + swapped(near), groups)
        (far, sides), state = lax.optimization_barrier(((far, sides), state))
        later = [(array, moved(above_steps, steps)) for array, steps in zip(sides, side_steps, strict=True)]
        later.append((join(far), [step for steps in above_steps for step in moved(corners, steps)]))
        others = swapped(later)
        state = fold(layout, queries, state, later, groups)
        return fold(layout, queries, state, others, groups, last=True)

    placed = P(AXES, None)
    return jax.shard_map(
        per_device, mesh=mesh, in_specs=(placed, placed, placed), out_specs=placed, check_vma=False
    )
```

```python
import functools
import math

import jax
import jax.numpy as jnp
from jax import lax
from jax.experimental import pallas as pl
from jax.experimental.pallas import tpu as pltpu
from jax.sharding import PartitionSpec as P

HD = 128
AXES = ("ctx", "kvh")
CORES = 2
HIDDEN = -1e30


class Layout:
    def __init__(self, mesh_shape):
        ctx, self.across = mesh_shape["ctx"], mesh_shape["kvh"]
        self.lines = 2
        self.planes = ctx // (CORES * self.lines)
        self.size = ctx * self.across

    def split(self, rank):
        column = rank % self.across
        core = rank // self.across % CORES
        line = rank // (self.across * CORES) % self.lines
        plane = rank // (self.across * CORES * self.lines)
        return plane, line, core, column

    def join(self, plane, line, core, column):
        return ((plane * self.lines + line) * CORES + core) * self.across + column

    def partner(self, rank, up=0, line=0, swap=0, column=0):
        place = self.split(rank)
        return self.join(place[0] ^ up, place[1] ^ line, place[2] ^ swap, place[3] ^ column)

    def exchange(self, array, **steps):
        return lax.ppermute(array, AXES, [(rank, self.partner(rank, **steps)) for rank in range(self.size)])

    def here(self):
        return lax.axis_index("ctx") * self.across + lax.axis_index("kvh")


def fold_kernel(layout, sources, rows, groups, carried, last, *refs):
    refs = list(refs)
    query_ref = refs.pop(0)
    state_refs = [refs.pop(0) for _ in range(3)] if carried else None
    piece_refs, refs = refs[: len(sources)], refs[len(sources) :]
    out_refs, (score_ref, weight_ref) = refs[:-2], refs[-2:]
    blocks = [steps for piece in sources for steps in piece]
    width = len(blocks) * rows
    heads = query_ref.shape[1] // (groups * HD)
    tall = heads * rows
    scale = math.log2(math.e) / math.sqrt(HD)

    rank = layout.here()
    along = lax.broadcasted_iota(jnp.int32, (1, width), 1)
    bias = jnp.zeros((1, width), jnp.float32)
    for at, (up, line, swap, column) in enumerate(blocks):
        hidden = layout.partner(rank, up, line, swap, column) > rank
        bias = jnp.where(along // rows == at, jnp.where(hidden, HIDDEN, 0.0).astype(jnp.float32), bias)
    own = blocks.index((0, 0, 0, 0)) * rows if (0, 0, 0, 0) in blocks else None
    if own is not None:
        token = lax.broadcasted_iota(jnp.int32, (rows, width), 0)
        place = lax.broadcasted_iota(jnp.int32, (rows, width), 1) - own
        later = jnp.logical_and(place < rows, place > token)
        bias = jnp.where(jnp.logical_and(place >= 0, later), HIDDEN, bias)

    for group in range(groups):
        first = group * heads * HD
        query = jnp.concatenate([query_ref[:, first + h * HD : first + (h + 1) * HD] for h in range(heads)], axis=0)
        at = group * HD
        key = jnp.concatenate([ref[:, at : at + HD] for ref in piece_refs], axis=0)
        at = (groups + group) * HD
        value = jnp.concatenate([ref[:, at : at + HD] for ref in piece_refs], axis=0)
        score_ref[...] = lax.dot_general(
            query, key, (((1,), (1,)), ((), ())), preferred_element_type=jnp.float32
        )
        tops, sums = [], []
        for begin in range(0, tall, rows):
            scores = score_ref[begin : begin + rows, :] * scale + bias
            top = jnp.broadcast_to(jnp.max(scores, axis=1, keepdims=True), (rows, HD))
            if carried:
                top = jnp.maximum(top, state_refs[0][group, begin : begin + rows])
            total = jnp.zeros((rows, HD), jnp.float32)
            rest = jnp.zeros((rows, 1), jnp.float32)
            for left in range(0, width, HD):
                part = min(HD, width - left)
                weights = jnp.exp2(scores[:, left : left + part] - top[:, :part])
                if part == HD:
                    total = total + weights
                else:
                    rest = jnp.sum(weights, axis=1, keepdims=True)
                weight_ref[begin : begin + rows, left : left + part] = weights.astype(jnp.bfloat16)
            tops.append(top)
            sums.append(jnp.broadcast_to(jnp.sum(total, axis=1, keepdims=True) + rest, (rows, HD)))
        largest, totals = jnp.concatenate(tops, axis=0), jnp.concatenate(sums, axis=0)
        summed = jnp.dot(weight_ref[...], value, preferred_element_type=jnp.float32)
        if carried:
            decay = jnp.exp2(state_refs[0][group] - largest)
            totals = totals + state_refs[1][group] * decay
            summed = summed + state_refs[2][group] * decay
        if last:
            result = (summed / totals).astype(jnp.bfloat16)
            for h in range(heads):
                out_refs[0][:, first + h * HD : first + (h + 1) * HD] = result[h * rows : (h + 1) * rows]
        else:
            for ref, array in zip(out_refs, (largest, totals, summed), strict=True):
                ref[group] = array


def fold(layout, queries, state, pieces, groups, last=False):
    rows, query_width = queries.shape
    tall = rows * query_width // (groups * HD)
    arrays = [array for array, _ in pieces]
    tokens = sum(array.shape[0] for array in arrays)
    carried = state is not None
    state_type = jax.ShapeDtypeStruct((groups, tall, HD), jnp.float32)
    whole = pl.BlockSpec(memory_space=pltpu.VMEM)
    return pl.pallas_call(
        functools.partial(
            fold_kernel, layout, [blocks for _, blocks in pieces], rows, groups, carried, last
        ),
        in_specs=[whole] * (1 + 3 * carried + len(arrays)),
        out_specs=whole if last else [whole] * 3,
        out_shape=jax.ShapeDtypeStruct(queries.shape, jnp.bfloat16) if last else [state_type] * 3,
        scratch_shapes=[pltpu.VMEM((tall, tokens), jnp.float32), pltpu.VMEM((tall, tokens), jnp.bfloat16)],
        compiler_params=pltpu.CompilerParams(vmem_limit_bytes=24 * 1024 * 1024),
        cost_estimate=pl.CostEstimate(flops=0, bytes_accessed=0, transcendentals=0),
    )(queries, *(state or ()), *arrays)


def solution(mesh):
    layout = Layout(dict(mesh.shape))

    def per_device(queries, keys, values):
        groups = keys.shape[1] // HD
        exchange = layout.exchange
        block = jnp.concatenate([keys, values], axis=1)
        ups = range(1, layout.planes)
        lines = range(1, layout.lines)
        columns = range(1, layout.across)
        side_steps = [(0, l, 0, 0) for l in lines] + [(0, 0, 0, c) for c in columns]
        corner_steps = [(0, l, 0, c) for l in lines for c in columns]
        above_steps = [(up, 0, 0, 0) for up in reversed(ups)]

        def go(array, steps):
            return exchange(array, up=steps[0], line=steps[1], swap=steps[2], column=steps[3])

        def moved(steps, by):
            return [tuple(a ^ b for a, b in zip(one, by, strict=True)) for one in steps]

        def swapped(pieces):
            return [(exchange(array, swap=1), moved(steps, (0, 0, 1, 0))) for array, steps in pieces]

        corner = [go(block, steps) for steps in corner_steps]
        corner = jnp.concatenate(corner, axis=0) if len(corner) > 1 else corner[0]
        tower_steps = [(0, 0, 0, 0)] + above_steps
        corner, above = lax.optimization_barrier((corner, [go(block, steps) for steps in above_steps]))
        near = [(jnp.concatenate([block] + above, axis=0), tower_steps)]
        far = [(corner, corner_steps)]
        far += [(go(corner, steps), moved(corner_steps, steps)) for steps in above_steps]
        sides = [(go(near[0][0], steps), moved(tower_steps, steps)) for steps in side_steps]

        def after(pieces, state):
            arrays, state = lax.optimization_barrier(([array for array, _ in pieces], state))
            return [(array, steps) for array, (_, steps) in zip(arrays, pieces, strict=True)], state

        state = fold(layout, queries, None, near, groups)
        near_others = swapped(near)
        state = fold(layout, queries, state, near_others, groups)
        far, state = after(far, state)
        far = [(jnp.concatenate([x for x, _ in far], axis=0), [one for _, steps in far for one in steps])]
        far_others = swapped(far)
        sides, state = after(sides, state)
        state = fold(layout, queries, state, far + sides, groups)
        return fold(layout, queries, state, swapped(sides) + far_others, groups, last=True)

    placed = P(AXES, None)
    return jax.shard_map(
        per_device, mesh=mesh, in_specs=(placed, placed, placed), out_specs=placed, check_vma=False
    )
```

```python
import functools
import math

import jax
import jax.numpy as jnp
from jax import lax
from jax.experimental import pallas as pl
from jax.experimental.pallas import tpu as pltpu
from jax.sharding import PartitionSpec as P

HD = 128
AXES = ("ctx", "kvh")
CORES = 2
HIDDEN = -1e30


class Layout:
    def __init__(self, mesh_shape):
        ctx, self.across = mesh_shape["ctx"], mesh_shape["kvh"]
        self.lines = 2
        self.planes = ctx // (CORES * self.lines)
        self.size = ctx * self.across

    def split(self, rank):
        column = rank % self.across
        core = rank // self.across % CORES
        line = rank // (self.across * CORES) % self.lines
        plane = rank // (self.across * CORES * self.lines)
        return plane, line, core, column

    def join(self, plane, line, core, column):
        return ((plane * self.lines + line) * CORES + core) * self.across + column

    def partner(self, rank, up=0, line=0, swap=0, column=0):
        place = self.split(rank)
        return self.join(place[0] ^ up, place[1] ^ line, place[2] ^ swap, place[3] ^ column)

    def exchange(self, array, **steps):
        return lax.ppermute(array, AXES, [(rank, self.partner(rank, **steps)) for rank in range(self.size)])

    def here(self):
        return lax.axis_index("ctx") * self.across + lax.axis_index("kvh")


def fold_kernel(layout, sources, rows, groups, carried, last, *refs):
    plane = layout.split(layout.here())[0]
    level = [[steps for steps in piece if steps[0] == 0] for piece in sources]
    assert all(piece[: len(flat)] == flat for piece, flat in zip(sources, level, strict=True))
    if level == sources:
        fold_blocks(layout, sources, rows, groups, carried, last, *refs)
        return

    @pl.when(plane == 0)
    def _():
        fold_blocks(layout, level, rows, groups, carried, last, *refs)

    @pl.when(plane > 0)
    def _():
        fold_blocks(layout, sources, rows, groups, carried, last, *refs)


def fold_blocks(layout, sources, rows, groups, carried, last, *refs):
    refs = list(refs)
    query_ref = refs.pop(0)
    state_refs = [refs.pop(0) for _ in range(3)] if carried else None
    piece_refs, refs = refs[: len(sources)], refs[len(sources) :]
    out_refs, (score_ref, weight_ref) = refs[:-2], refs[-2:]
    blocks = [steps for piece in sources for steps in piece]
    taken = [(ref, len(piece) * rows) for ref, piece in zip(piece_refs, sources, strict=True) if piece]
    width = len(blocks) * rows
    heads = query_ref.shape[1] // (groups * HD)
    tall = heads * rows
    scale = math.log2(math.e) / math.sqrt(HD)

    rank = layout.here()
    along = lax.broadcasted_iota(jnp.int32, (1, width), 1)
    bias = jnp.zeros((1, width), jnp.float32)
    for at, (up, line, swap, column) in enumerate(blocks):
        hidden = layout.partner(rank, up, line, swap, column) > rank
        bias = jnp.where(along // rows == at, jnp.where(hidden, HIDDEN, 0.0).astype(jnp.float32), bias)
    own = blocks.index((0, 0, 0, 0)) * rows if (0, 0, 0, 0) in blocks else None
    if own is not None:
        token = lax.broadcasted_iota(jnp.int32, (rows, width), 0)
        place = lax.broadcasted_iota(jnp.int32, (rows, width), 1) - own
        later = jnp.logical_and(place < rows, place > token)
        bias = jnp.where(jnp.logical_and(place >= 0, later), HIDDEN, bias)

    def score(group):
        first = group * heads * HD
        query = jnp.concatenate([query_ref[:, first + h * HD : first + (h + 1) * HD] for h in range(heads)], axis=0)
        at = group * HD
        key = jnp.concatenate([ref[:size, at : at + HD] for ref, size in taken], axis=0)
        score_ref[group % 2, :, :width] = lax.dot_general(
            query, key, (((1,), (1,)), ((), ())), preferred_element_type=jnp.float32
        )

    def mix(group):
        slot = group % 2
        tops, sums = [], []
        for begin in range(0, tall, rows):
            scores = score_ref[slot, begin : begin + rows, :width] * scale + bias
            top = jnp.broadcast_to(jnp.max(scores, axis=1, keepdims=True), (rows, HD))
            if carried:
                top = jnp.maximum(top, state_refs[0][group, begin : begin + rows])
            total = jnp.zeros((rows, HD), jnp.float32)
            rest = jnp.zeros((rows, 1), jnp.float32)
            for left in range(0, width, HD):
                part = min(HD, width - left)
                weights = jnp.exp2(scores[:, left : left + part] - top[:, :part])
                if part == HD:
                    total = total + weights
                else:
                    rest = jnp.sum(weights, axis=1, keepdims=True)
                weight_ref[slot, begin : begin + rows, left : left + part] = weights.astype(jnp.bfloat16)
            tops.append(top)
            sums.append(jnp.broadcast_to(jnp.sum(total, axis=1, keepdims=True) + rest, (rows, HD)))
        largest, totals = jnp.concatenate(tops, axis=0), jnp.concatenate(sums, axis=0)
        at = (groups + group) * HD
        value = jnp.concatenate([ref[:size, at : at + HD] for ref, size in taken], axis=0)
        summed = jnp.dot(weight_ref[slot, :, :width], value, preferred_element_type=jnp.float32)
        if carried:
            decay = jnp.exp2(state_refs[0][group] - largest)
            totals = totals + state_refs[1][group] * decay
            summed = summed + state_refs[2][group] * decay
        if last:
            first = group * heads * HD
            result = (summed / totals).astype(jnp.bfloat16)
            for h in range(heads):
                out_refs[0][:, first + h * HD : first + (h + 1) * HD] = result[h * rows : (h + 1) * rows]
        else:
            for ref, array in zip(out_refs, (largest, totals, summed), strict=True):
                ref[group] = array

    for begin in range(0, groups, 2):
        both = range(begin, min(begin + 2, groups))
        for group in both:
            score(group)
        for group in both:
            mix(group)


def fold(layout, queries, state, pieces, groups, last=False):
    rows, query_width = queries.shape
    tall = rows * query_width // (groups * HD)
    arrays = [array for array, _ in pieces]
    tokens = -(-sum(array.shape[0] for array in arrays) // HD) * HD
    carried = state is not None
    state_type = jax.ShapeDtypeStruct((groups, tall, HD), jnp.float32)
    whole = pl.BlockSpec(memory_space=pltpu.VMEM)
    return pl.pallas_call(
        functools.partial(
            fold_kernel, layout, [blocks for _, blocks in pieces], rows, groups, carried, last
        ),
        in_specs=[whole] * (1 + 3 * carried + len(arrays)),
        out_specs=whole if last else [whole] * 3,
        out_shape=jax.ShapeDtypeStruct(queries.shape, jnp.bfloat16) if last else [state_type] * 3,
        scratch_shapes=[pltpu.VMEM((2, tall, tokens), jnp.float32), pltpu.VMEM((2, tall, tokens), jnp.bfloat16)],
        compiler_params=pltpu.CompilerParams(vmem_limit_bytes=24 * 1024 * 1024),
        cost_estimate=pl.CostEstimate(flops=0, bytes_accessed=0, transcendentals=0),
    )(queries, *(state or ()), *arrays)


def solution(mesh):
    layout = Layout(dict(mesh.shape))

    def per_device(queries, keys, values):
        groups = keys.shape[1] // HD
        exchange = layout.exchange
        block = jnp.concatenate([keys, values], axis=1)
        ups = range(1, layout.planes)
        lines = range(1, layout.lines)
        columns = range(1, layout.across)
        side_steps = [(0, l, 0, 0) for l in lines] + [(0, 0, 0, c) for c in columns]
        corner_steps = [(0, l, 0, c) for l in lines for c in columns]
        above_steps = [(up, 0, 0, 0) for up in reversed(ups)]

        def go(array, steps):
            return exchange(array, up=steps[0], line=steps[1], swap=steps[2], column=steps[3])

        def moved(steps, by):
            return [tuple(a ^ b for a, b in zip(one, by, strict=True)) for one in steps]

        def swapped(pieces):
            return [(exchange(array, swap=1), moved(steps, (0, 0, 1, 0))) for array, steps in pieces]

        corner = [go(block, steps) for steps in corner_steps]
        corner = jnp.concatenate(corner, axis=0) if len(corner) > 1 else corner[0]
        tower_steps = [(0, 0, 0, 0)] + above_steps
        corner, above = lax.optimization_barrier((corner, [go(block, steps) for steps in above_steps]))
        near = [(jnp.concatenate([block] + above, axis=0), tower_steps)]
        far = [(corner, corner_steps)]
        far += [(go(corner, steps), moved(corner_steps, steps)) for steps in above_steps]
        sides = [(go(near[0][0], steps), moved(tower_steps, steps)) for steps in side_steps]

        def after(pieces, state):
            arrays, state = lax.optimization_barrier(([array for array, _ in pieces], state))
            return [(array, steps) for array, (_, steps) in zip(arrays, pieces, strict=True)], state

        state = fold(layout, queries, None, near, groups)
        sides, state = after(sides, state)
        others = swapped(near) + swapped(sides)
        state = fold(layout, queries, state, sides, groups)
        far, state = after(far, state)
        far = [(jnp.concatenate([x for x, _ in far], axis=0), [one for _, steps in far for one in steps])]
        far_others = swapped(far)
        state = fold(layout, queries, state, others, groups)
        return fold(layout, queries, state, far + far_others, groups, last=True)

    placed = P(AXES, None)
    return jax.shard_map(
        per_device, mesh=mesh, in_specs=(placed, placed, placed), out_specs=placed, check_vma=False
    )
```

```python
import functools
import math

import jax
import jax.numpy as jnp
from jax import lax
from jax.experimental import pallas as pl
from jax.experimental.pallas import tpu as pltpu
from jax.sharding import PartitionSpec as P

HD = 128
AXES = ("ctx", "kvh")
CORES = 2
HIDDEN = -1e30
HERE = (0, 0)
SELF = (HERE, 0, 0, 0)


class Layout:
    def __init__(self, mesh_shape):
        ctx, self.across = mesh_shape["ctx"], mesh_shape["kvh"]
        self.lines = 2
        self.planes = ctx // (CORES * self.lines)
        self.size = ctx * self.across

    def split(self, rank):
        column = rank % self.across
        core = rank // self.across % CORES
        line = rank // (self.across * CORES) % self.lines
        plane = rank // (self.across * CORES * self.lines)
        return plane, line, core, column

    def join(self, plane, line, core, column):
        return ((plane * self.lines + line) * CORES + core) * self.across + column

    def partner(self, rank, steps):
        (even, odd), line, swap, column = steps
        place = self.split(rank)
        up = even * (1 - place[2]) + odd * place[2]
        return self.join(place[0] ^ up, place[1] ^ line, place[2] ^ swap, place[3] ^ column)

    def exchange(self, array, steps):
        return lax.ppermute(array, AXES, [(rank, self.partner(rank, steps)) for rank in range(self.size)])

    def here(self):
        return lax.axis_index("ctx") * self.across + lax.axis_index("kvh")


def fold_kernel(layout, sources, rows, groups, carried, last, *refs):
    plane = layout.split(layout.here())[0]
    level = [[steps for steps in piece if steps[0] == HERE] for piece in sources]
    assert all(piece[: len(flat)] == flat for piece, flat in zip(sources, level, strict=True))
    if level == sources:
        fold_blocks(layout, sources, rows, groups, carried, last, *refs)
        return

    @pl.when(plane == 0)
    def _():
        fold_blocks(layout, level, rows, groups, carried, last, *refs)

    @pl.when(plane > 0)
    def _():
        fold_blocks(layout, sources, rows, groups, carried, last, *refs)


def fold_blocks(layout, sources, rows, groups, carried, last, *refs):
    refs = list(refs)
    query_ref = refs.pop(0)
    state_refs = [refs.pop(0) for _ in range(3)] if carried else None
    piece_refs, refs = refs[: len(sources)], refs[len(sources) :]
    out_refs, (score_ref, weight_ref) = refs[:-2], refs[-2:]
    blocks = [steps for piece in sources for steps in piece]
    taken = [(ref, len(piece) * rows) for ref, piece in zip(piece_refs, sources, strict=True) if piece]
    width = len(blocks) * rows
    heads = query_ref.shape[1] // (groups * HD)
    tall = heads * rows
    scale = math.log2(math.e) / math.sqrt(HD)

    rank = layout.here()
    along = lax.broadcasted_iota(jnp.int32, (1, width), 1)
    bias = jnp.zeros((1, width), jnp.float32)
    for at, steps in enumerate(blocks):
        hidden = layout.partner(rank, steps) > rank
        bias = jnp.where(along // rows == at, jnp.where(hidden, HIDDEN, 0.0).astype(jnp.float32), bias)
    own = blocks.index(SELF) * rows if SELF in blocks else None
    if own is not None:
        token = lax.broadcasted_iota(jnp.int32, (rows, width), 0)
        place = lax.broadcasted_iota(jnp.int32, (rows, width), 1) - own
        later = jnp.logical_and(place < rows, place > token)
        bias = jnp.where(jnp.logical_and(place >= 0, later), HIDDEN, bias)

    def write(group, largest, totals, summed):
        if last:
            first = group * heads * HD
            result = (summed / totals).astype(jnp.bfloat16)
            for h in range(heads):
                out_refs[0][:, first + h * HD : first + (h + 1) * HD] = result[h * rows : (h + 1) * rows]
        else:
            for ref, array in zip(out_refs, (largest, totals, summed), strict=True):
                ref[group] = array

    if not blocks:
        for group in range(groups):
            write(group, *(ref[group] for ref in state_refs))
        return

    def score(group):
        first = group * heads * HD
        query = jnp.concatenate([query_ref[:, first + h * HD : first + (h + 1) * HD] for h in range(heads)], axis=0)
        at = group * HD
        key = jnp.concatenate([ref[:size, at : at + HD] for ref, size in taken], axis=0)
        score_ref[group % 2, :, :width] = lax.dot_general(
            query, key, (((1,), (1,)), ((), ())), preferred_element_type=jnp.float32
        )

    def mix(group):
        slot = group % 2
        tops, sums = [], []
        for begin in range(0, tall, rows):
            scores = score_ref[slot, begin : begin + rows, :width] * scale + bias
            top = jnp.broadcast_to(jnp.max(scores, axis=1, keepdims=True), (rows, HD))
            if carried:
                top = jnp.maximum(top, state_refs[0][group, begin : begin + rows])
            total = jnp.zeros((rows, HD), jnp.float32)
            rest = jnp.zeros((rows, 1), jnp.float32)
            for left in range(0, width, HD):
                part = min(HD, width - left)
                weights = jnp.exp2(scores[:, left : left + part] - top[:, :part])
                if part == HD:
                    total = total + weights
                else:
                    rest = jnp.sum(weights, axis=1, keepdims=True)
                weight_ref[slot, begin : begin + rows, left : left + part] = weights.astype(jnp.bfloat16)
            tops.append(top)
            sums.append(jnp.broadcast_to(jnp.sum(total, axis=1, keepdims=True) + rest, (rows, HD)))
        largest, totals = jnp.concatenate(tops, axis=0), jnp.concatenate(sums, axis=0)
        at = (groups + group) * HD
        value = jnp.concatenate([ref[:size, at : at + HD] for ref, size in taken], axis=0)
        summed = jnp.dot(weight_ref[slot, :, :width], value, preferred_element_type=jnp.float32)
        if carried:
            decay = jnp.exp2(state_refs[0][group] - largest)
            totals = totals + state_refs[1][group] * decay
            summed = summed + state_refs[2][group] * decay
        write(group, largest, totals, summed)

    for begin in range(0, groups, 2):
        both = range(begin, min(begin + 2, groups))
        for group in both:
            score(group)
        for group in both:
            mix(group)


def fold(layout, queries, state, pieces, groups, last=False):
    rows, query_width = queries.shape
    tall = rows * query_width // (groups * HD)
    arrays = [array for array, _ in pieces]
    tokens = -(-sum(array.shape[0] for array in arrays) // HD) * HD
    carried = state is not None
    state_type = jax.ShapeDtypeStruct((groups, tall, HD), jnp.float32)
    whole = pl.BlockSpec(memory_space=pltpu.VMEM)
    return pl.pallas_call(
        functools.partial(
            fold_kernel, layout, [blocks for _, blocks in pieces], rows, groups, carried, last
        ),
        in_specs=[whole] * (1 + 3 * carried + len(arrays)),
        out_specs=whole if last else [whole] * 3,
        out_shape=jax.ShapeDtypeStruct(queries.shape, jnp.bfloat16) if last else [state_type] * 3,
        scratch_shapes=[pltpu.VMEM((2, tall, tokens), jnp.float32), pltpu.VMEM((2, tall, tokens), jnp.bfloat16)],
        compiler_params=pltpu.CompilerParams(vmem_limit_bytes=24 * 1024 * 1024),
        cost_estimate=pl.CostEstimate(flops=0, bytes_accessed=0, transcendentals=0),
    )(queries, *(state or ()), *arrays)


def solution(mesh):
    layout = Layout(dict(mesh.shape))

    def per_device(queries, keys, values):
        groups = keys.shape[1] // HD
        go = layout.exchange
        block = jnp.concatenate([keys, values], axis=1)
        ups = list(range(layout.planes - 1, 0, -1))
        lines = range(1, layout.lines)
        columns = range(1, layout.across)
        side_steps = [(HERE, l, 0, 0) for l in lines] + [(HERE, 0, 0, c) for c in columns]
        corner_steps = [(HERE, l, 0, c) for l in lines for c in columns]
        above_steps = [((up, up), 0, 0, 0) for up in ups]
        if layout.planes == 4:
            above_steps = [(pair, 0, 0, 0) for pair in [(3, 3), (2, 2), (1, 1)]]
        far_above = [(pair, 0, 0, 0) for pair in [(3, 3), (2, 2), (1, 1)]] if layout.planes == 4 else above_steps
        tower_steps = [SELF] + above_steps

        def moved(steps, by):
            def add(one):
                up = (one[0][0] ^ by[0][0], one[0][1] ^ by[0][1])
                return up, one[1] ^ by[1], one[2] ^ by[2], one[3] ^ by[3]

            return [add(one) for one in steps]

        def swapped(pieces):
            turned = [(go(array, (HERE, 0, 1, 0)), steps) for array, steps in pieces]
            return [(array, [(up[::-1], l, 1 - swap, c) for up, l, swap, c in steps]) for array, steps in turned]

        def join(pieces):
            if len(pieces) == 1:
                return pieces[0]
            return jnp.concatenate([x for x, _ in pieces], axis=0), [one for _, steps in pieces for one in steps]

        def after(pieces, state):
            arrays, state = lax.optimization_barrier(([array for array, _ in pieces], state))
            return [(array, steps) for array, (_, steps) in zip(arrays, pieces, strict=True)], state

        corner = join([(go(block, steps), [steps]) for steps in corner_steps])
        corner_array, above = lax.optimization_barrier((corner[0], [go(block, steps) for steps in above_steps]))
        corner = (corner_array, corner[1])
        near = [(jnp.concatenate([block] + above, axis=0), tower_steps)]
        sides = [(go(near[0][0], steps), moved(tower_steps, steps)) for steps in side_steps]
        far = [corner] + [(go(corner[0], steps), moved(corner[1], steps)) for steps in far_above]

        state = fold(layout, queries, None, near, groups)
        sides, state = after(sides, state)
        side_others = swapped(sides)
        state = fold(layout, queries, state, sides, groups)
        rest, state = after(far + near, state)
        far, near = rest[:-1], rest[-1:]
        far = [join(far)]
        others = swapped(far) + swapped(near)
        state = fold(layout, queries, state, side_others + far, groups)
        return fold(layout, queries, state, others, groups, last=True)

    placed = P(AXES, None)
    return jax.shard_map(
        per_device, mesh=mesh, in_specs=(placed, placed, placed), out_specs=placed, check_vma=False
    )
```

```python
import functools
import math

import jax
import jax.numpy as jnp
from jax import lax
from jax.experimental import pallas as pl
from jax.experimental.pallas import tpu as pltpu
from jax.sharding import PartitionSpec as P

HD = 128
AXES = ("ctx", "kvh")
CORES = 2
HIDDEN = -1e30
HERE = (0, 0)
SELF = (HERE, 0, 0, 0)


class Layout:
    def __init__(self, mesh_shape):
        ctx, self.across = mesh_shape["ctx"], mesh_shape["kvh"]
        self.lines = 2
        self.planes = ctx // (CORES * self.lines)
        self.size = ctx * self.across

    def split(self, rank):
        column = rank % self.across
        core = rank // self.across % CORES
        line = rank // (self.across * CORES) % self.lines
        plane = rank // (self.across * CORES * self.lines)
        return plane, line, core, column

    def join(self, plane, line, core, column):
        return ((plane * self.lines + line) * CORES + core) * self.across + column

    def partner(self, rank, steps):
        (even, odd), line, swap, column = steps
        place = self.split(rank)
        up = even * (1 - place[2]) + odd * place[2]
        return self.join(place[0] ^ up, place[1] ^ line, place[2] ^ swap, place[3] ^ column)

    def exchange(self, array, steps):
        return lax.ppermute(array, AXES, [(rank, self.partner(rank, steps)) for rank in range(self.size)])

    def here(self):
        return lax.axis_index("ctx") * self.across + lax.axis_index("kvh")


def fold_kernel(layout, sources, rows, groups, carried, last, *refs):
    plane = layout.split(layout.here())[0]
    assert all(piece == sorted(piece, key=lambda steps: max(steps[0])) for piece in sources)

    def upto(most):
        return [[steps for steps in piece if max(steps[0]) <= most] for piece in sources]

    def run(taken):
        fold_blocks(layout, taken, rows, groups, carried, last, *refs)

    if upto(0) == sources:
        run(sources)
        return
    pl.when(plane == 0)(lambda: run(upto(0)))
    if layout.planes > 2:
        pl.when(plane == 1)(lambda: run(upto(1)))
        pl.when(plane > 1)(lambda: run(sources))
    else:
        pl.when(plane == 1)(lambda: run(sources))


def fold_blocks(layout, sources, rows, groups, carried, last, *refs):
    refs = list(refs)
    query_ref = refs.pop(0)
    state_refs = [refs.pop(0) for _ in range(3)] if carried else None
    piece_refs, refs = refs[: len(sources)], refs[len(sources) :]
    out_refs, (score_ref, weight_ref) = refs[:-2], refs[-2:]
    blocks = [steps for piece in sources for steps in piece]
    taken = [(ref, len(piece) * rows) for ref, piece in zip(piece_refs, sources, strict=True) if piece]
    width = len(blocks) * rows
    heads = query_ref.shape[1] // (groups * HD)
    tall = heads * rows
    scale = math.log2(math.e) / math.sqrt(HD)

    rank = layout.here()
    along = lax.broadcasted_iota(jnp.int32, (1, width), 1)
    bias = jnp.zeros((1, width), jnp.float32)
    for at, steps in enumerate(blocks):
        hidden = layout.partner(rank, steps) > rank
        bias = jnp.where(along // rows == at, jnp.where(hidden, HIDDEN, 0.0).astype(jnp.float32), bias)
    own = blocks.index(SELF) * rows if SELF in blocks else None
    if own is not None:
        token = lax.broadcasted_iota(jnp.int32, (rows, width), 0)
        place = lax.broadcasted_iota(jnp.int32, (rows, width), 1) - own
        later = jnp.logical_and(place < rows, place > token)
        bias = jnp.where(jnp.logical_and(place >= 0, later), HIDDEN, bias)

    def write(group, largest, totals, summed):
        if last:
            first = group * heads * HD
            result = (summed / totals).astype(jnp.bfloat16)
            for h in range(heads):
                out_refs[0][:, first + h * HD : first + (h + 1) * HD] = result[h * rows : (h + 1) * rows]
        else:
            for ref, array in zip(out_refs, (largest, totals, summed), strict=True):
                ref[group] = array

    if not blocks:
        for group in range(groups):
            write(group, *(ref[group] for ref in state_refs))
        return

    def score(group):
        first = group * heads * HD
        query = jnp.concatenate([query_ref[:, first + h * HD : first + (h + 1) * HD] for h in range(heads)], axis=0)
        at = group * HD
        key = jnp.concatenate([ref[:size, at : at + HD] for ref, size in taken], axis=0)
        score_ref[group % 2, :, :width] = lax.dot_general(
            query, key, (((1,), (1,)), ((), ())), preferred_element_type=jnp.float32
        )

    def mix(group):
        slot = group % 2
        tops, sums = [], []
        for begin in range(0, tall, rows):
            scores = score_ref[slot, begin : begin + rows, :width] * scale + bias
            top = jnp.broadcast_to(jnp.max(scores, axis=1, keepdims=True), (rows, HD))
            if carried:
                top = jnp.maximum(top, state_refs[0][group, begin : begin + rows])
            total = jnp.zeros((rows, HD), jnp.float32)
            rest = jnp.zeros((rows, 1), jnp.float32)
            for left in range(0, width, HD):
                part = min(HD, width - left)
                weights = jnp.exp2(scores[:, left : left + part] - top[:, :part])
                if part == HD:
                    total = total + weights
                else:
                    rest = jnp.sum(weights, axis=1, keepdims=True)
                weight_ref[slot, begin : begin + rows, left : left + part] = weights.astype(jnp.bfloat16)
            tops.append(top)
            sums.append(jnp.broadcast_to(jnp.sum(total, axis=1, keepdims=True) + rest, (rows, HD)))
        largest, totals = jnp.concatenate(tops, axis=0), jnp.concatenate(sums, axis=0)
        at = (groups + group) * HD
        value = jnp.concatenate([ref[:size, at : at + HD] for ref, size in taken], axis=0)
        summed = jnp.dot(weight_ref[slot, :, :width], value, preferred_element_type=jnp.float32)
        if carried:
            decay = jnp.exp2(state_refs[0][group] - largest)
            totals = totals + state_refs[1][group] * decay
            summed = summed + state_refs[2][group] * decay
        write(group, largest, totals, summed)

    for begin in range(0, groups, 2):
        both = range(begin, min(begin + 2, groups))
        for group in both:
            score(group)
        for group in both:
            mix(group)


def fold(layout, queries, state, pieces, groups, last=False):
    rows, query_width = queries.shape
    tall = rows * query_width // (groups * HD)
    arrays = [array for array, _ in pieces]
    tokens = -(-sum(array.shape[0] for array in arrays) // HD) * HD
    carried = state is not None
    state_type = jax.ShapeDtypeStruct((groups, tall, HD), jnp.float32)
    whole = pl.BlockSpec(memory_space=pltpu.VMEM)
    return pl.pallas_call(
        functools.partial(
            fold_kernel, layout, [blocks for _, blocks in pieces], rows, groups, carried, last
        ),
        in_specs=[whole] * (1 + 3 * carried + len(arrays)),
        out_specs=whole if last else [whole] * 3,
        out_shape=jax.ShapeDtypeStruct(queries.shape, jnp.bfloat16) if last else [state_type] * 3,
        scratch_shapes=[pltpu.VMEM((2, tall, tokens), jnp.float32), pltpu.VMEM((2, tall, tokens), jnp.bfloat16)],
        compiler_params=pltpu.CompilerParams(vmem_limit_bytes=24 * 1024 * 1024),
        cost_estimate=pl.CostEstimate(flops=0, bytes_accessed=0, transcendentals=0),
    )(queries, *(state or ()), *arrays)


def solution(mesh):
    layout = Layout(dict(mesh.shape))

    def per_device(queries, keys, values):
        groups = keys.shape[1] // HD
        go = layout.exchange
        block = jnp.concatenate([keys, values], axis=1)
        above = [((up, up), 0, 0, 0) for up in range(layout.planes - 1, 0, -1)]
        columns = [(HERE, 0, 0, c) for c in range(1, layout.across)]
        lines = [(HERE, l, 0, 0) for l in range(1, layout.lines)]
        corners = [(HERE, l, 0, c) for _, l, _, _ in lines for _, _, _, c in columns]

        def moved(steps, by):
            def add(one):
                up = (one[0][0] ^ by[0][0], one[0][1] ^ by[0][1])
                return up, one[1] ^ by[1], one[2] ^ by[2], one[3] ^ by[3]

            return [add(one) for one in steps]

        def sent(piece, by):
            return go(piece[0], by), moved(piece[1], by)

        def swapped(pieces):
            turned = [sent(piece, (HERE, 0, 1, 0)) for piece in pieces]
            return [(array, [(up[::-1], l, swap, c) for up, l, swap, c in steps]) for array, steps in turned]

        def join(pieces):
            if len(pieces) == 1:
                return pieces[0]
            return jnp.concatenate([x for x, _ in pieces], axis=0), [one for _, steps in pieces for one in steps]

        def tied(pieces, state=None):
            arrays, state = lax.optimization_barrier(([array for array, _ in pieces], state))
            return [(array, steps) for array, (_, steps) in zip(arrays, pieces, strict=True)], state

        own = (block, [SELF])
        corner = join([sent(own, steps) for steps in corners])
        column = [sent(own, steps) for steps in above]
        (longest, corner, *column), _ = tied([column[0], corner, *column[1:]])
        near = join([own, *column[::-1], longest])
        (near, corner), _ = tied([near, corner])
        far = [sent(corner, steps) for steps in above]
        sides = [sent(near, steps) for steps in columns + lines]

        state = fold(layout, queries, None, [near, corner], groups)
        sides, state = tied(sides, state)
        others = swapped(sides) + swapped([join([corner, near])])
        state = fold(layout, queries, state, sides, groups)
        far, state = tied(far, state)
        far = [join(far[::-1])]
        far_others = swapped(far)
        state = fold(layout, queries, state, others, groups)
        return fold(layout, queries, state, far + far_others, groups, last=True)

    placed = P(AXES, None)
    return jax.shard_map(
        per_device, mesh=mesh, in_specs=(placed, placed, placed), out_specs=placed, check_vma=False
    )
```

```python
import functools
import math

import jax
import jax.numpy as jnp
from jax import lax
from jax.experimental import pallas as pl
from jax.experimental.pallas import tpu as pltpu
from jax.sharding import PartitionSpec as P

HD = 128
AXES = ("ctx", "kvh")
CORES = 2
HIDDEN = -1e30
HERE = (0, 0)
SELF = (HERE, 0, 0, 0)


class Layout:
    def __init__(self, mesh_shape):
        ctx, self.across = mesh_shape["ctx"], mesh_shape["kvh"]
        self.lines = 2
        self.planes = ctx // (CORES * self.lines)
        self.size = ctx * self.across

    def split(self, rank):
        column = rank % self.across
        core = rank // self.across % CORES
        line = rank // (self.across * CORES) % self.lines
        plane = rank // (self.across * CORES * self.lines)
        return plane, line, core, column

    def join(self, plane, line, core, column):
        return ((plane * self.lines + line) * CORES + core) * self.across + column

    def partner(self, rank, steps):
        (even, odd), line, swap, column = steps
        place = self.split(rank)
        up = even * (1 - place[2]) + odd * place[2]
        return self.join(place[0] ^ up, place[1] ^ line, place[2] ^ swap, place[3] ^ column)

    def exchange(self, array, steps):
        return lax.ppermute(array, AXES, [(rank, self.partner(rank, steps)) for rank in range(self.size)])

    def here(self):
        return lax.axis_index("ctx") * self.across + lax.axis_index("kvh")


def fold_kernel(layout, sources, rows, groups, carried, last, *refs):
    plane = layout.split(layout.here())[0]

    def run(ups):
        fold_blocks(layout, sources, rows, groups, carried, last, ups, *refs)

    every = {up for piece in sources for steps in piece for up in steps[0]}
    if every == {0}:
        run(every)
        return
    few = min(3, layout.planes - 1)
    for at in range(few):
        pl.when(plane == at)(functools.partial(run, {up for up in every if at ^ up <= at}))
    pl.when(plane >= few)(lambda: run(every))


def fold_blocks(layout, sources, rows, groups, carried, last, ups, *refs):
    refs = list(refs)
    query_ref = refs.pop(0)
    state_refs = [refs.pop(0) for _ in range(3)] if carried else None
    piece_refs, refs = refs[: len(sources)], refs[len(sources) :]
    out_refs, (score_ref, weight_ref) = refs[:-2], refs[-2:]
    blocks, runs = [], []
    for ref, piece in zip(piece_refs, sources, strict=True):
        for at, steps in enumerate(piece):
            if not ups.issuperset(steps[0]):
                continue
            blocks.append(steps)
            if runs and runs[-1][0] is ref and runs[-1][2] == at * rows:
                runs[-1][2] += rows
            else:
                runs.append([ref, at * rows, (at + 1) * rows])
    width = len(blocks) * rows
    heads = query_ref.shape[1] // (groups * HD)
    tall = heads * rows
    scale = math.log2(math.e) / math.sqrt(HD)

    rank = layout.here()
    along = lax.broadcasted_iota(jnp.int32, (1, width), 1)
    bias = jnp.zeros((1, width), jnp.float32)
    for at, steps in enumerate(blocks):
        hidden = layout.partner(rank, steps) > rank
        bias = jnp.where(along // rows == at, jnp.where(hidden, HIDDEN, 0.0).astype(jnp.float32), bias)
    own = blocks.index(SELF) * rows if SELF in blocks else None
    if own is not None:
        token = lax.broadcasted_iota(jnp.int32, (rows, width), 0)
        place = lax.broadcasted_iota(jnp.int32, (rows, width), 1) - own
        later = jnp.logical_and(place < rows, place > token)
        bias = jnp.where(jnp.logical_and(place >= 0, later), HIDDEN, bias)

    def write(group, largest, totals, summed):
        if last:
            first = group * heads * HD
            result = (summed / totals).astype(jnp.bfloat16)
            for h in range(heads):
                out_refs[0][:, first + h * HD : first + (h + 1) * HD] = result[h * rows : (h + 1) * rows]
        else:
            for ref, array in zip(out_refs, (largest, totals, summed), strict=True):
                ref[group] = array

    if not blocks:
        for group in range(groups):
            write(group, *(ref[group] for ref in state_refs))
        return

    def score(group):
        first = group * heads * HD
        query = jnp.concatenate([query_ref[:, first + h * HD : first + (h + 1) * HD] for h in range(heads)], axis=0)
        at = group * HD
        key = jnp.concatenate([ref[begin:end, at : at + HD] for ref, begin, end in runs], axis=0)
        score_ref[group % 2, :, :width] = lax.dot_general(
            query, key, (((1,), (1,)), ((), ())), preferred_element_type=jnp.float32
        )

    def mix(group):
        slot = group % 2
        tops, sums = [], []
        for begin in range(0, tall, rows):
            scores = score_ref[slot, begin : begin + rows, :width] * scale + bias
            top = jnp.broadcast_to(jnp.max(scores, axis=1, keepdims=True), (rows, HD))
            if carried:
                top = jnp.maximum(top, state_refs[0][group, begin : begin + rows])
            total = jnp.zeros((rows, HD), jnp.float32)
            rest = jnp.zeros((rows, 1), jnp.float32)
            for left in range(0, width, HD):
                part = min(HD, width - left)
                weights = jnp.exp2(scores[:, left : left + part] - top[:, :part])
                if part == HD:
                    total = total + weights
                else:
                    rest = jnp.sum(weights, axis=1, keepdims=True)
                weight_ref[slot, begin : begin + rows, left : left + part] = weights.astype(jnp.bfloat16)
            tops.append(top)
            sums.append(jnp.broadcast_to(jnp.sum(total, axis=1, keepdims=True) + rest, (rows, HD)))
        largest, totals = jnp.concatenate(tops, axis=0), jnp.concatenate(sums, axis=0)
        at = (groups + group) * HD
        value = jnp.concatenate([ref[begin:end, at : at + HD] for ref, begin, end in runs], axis=0)
        summed = jnp.dot(weight_ref[slot, :, :width], value, preferred_element_type=jnp.float32)
        if carried:
            decay = jnp.exp2(state_refs[0][group] - largest)
            totals = totals + state_refs[1][group] * decay
            summed = summed + state_refs[2][group] * decay
        write(group, largest, totals, summed)

    for begin in range(0, groups, 2):
        both = range(begin, min(begin + 2, groups))
        for group in both:
            score(group)
        for group in both:
            mix(group)


def fold(layout, queries, state, pieces, groups, last=False):
    rows, query_width = queries.shape
    tall = rows * query_width // (groups * HD)
    arrays = [array for array, _ in pieces]
    tokens = -(-sum(array.shape[0] for array in arrays) // HD) * HD
    carried = state is not None
    state_type = jax.ShapeDtypeStruct((groups, tall, HD), jnp.float32)
    whole = pl.BlockSpec(memory_space=pltpu.VMEM)
    return pl.pallas_call(
        functools.partial(
            fold_kernel, layout, [blocks for _, blocks in pieces], rows, groups, carried, last
        ),
        in_specs=[whole] * (1 + 3 * carried + len(arrays)),
        out_specs=whole if last else [whole] * 3,
        out_shape=jax.ShapeDtypeStruct(queries.shape, jnp.bfloat16) if last else [state_type] * 3,
        scratch_shapes=[pltpu.VMEM((2, tall, tokens), jnp.float32), pltpu.VMEM((2, tall, tokens), jnp.bfloat16)],
        compiler_params=pltpu.CompilerParams(vmem_limit_bytes=24 * 1024 * 1024),
        cost_estimate=pl.CostEstimate(flops=0, bytes_accessed=0, transcendentals=0),
    )(queries, *(state or ()), *arrays)


def solution(mesh):
    layout = Layout(dict(mesh.shape))

    def per_device(queries, keys, values):
        groups = keys.shape[1] // HD
        go = layout.exchange
        block = jnp.concatenate([keys, values], axis=1)
        above = [((up, up), 0, 0, 0) for up in range(layout.planes - 1, 0, -1)]
        columns = [(HERE, 0, 0, c) for c in range(1, layout.across)]
        lines = [(HERE, l, 0, 0) for l in range(1, layout.lines)]
        corners = [(HERE, l, 0, c) for _, l, _, _ in lines for _, _, _, c in columns]

        def moved(steps, by):
            def add(one):
                up = (one[0][0] ^ by[0][0], one[0][1] ^ by[0][1])
                return up, one[1] ^ by[1], one[2] ^ by[2], one[3] ^ by[3]

            return [add(one) for one in steps]

        def sent(piece, by):
            return go(piece[0], by), moved(piece[1], by)

        def swapped(pieces):
            turned = [sent(piece, (HERE, 0, 1, 0)) for piece in pieces]
            return [(array, [(up[::-1], l, swap, c) for up, l, swap, c in steps]) for array, steps in turned]

        def join(pieces):
            if len(pieces) == 1:
                return pieces[0]
            return jnp.concatenate([x for x, _ in pieces], axis=0), [one for _, steps in pieces for one in steps]

        def tied(pieces, state=None):
            arrays, state = lax.optimization_barrier(([array for array, _ in pieces], state))
            return [(array, steps) for array, (_, steps) in zip(arrays, pieces, strict=True)], state

        own = (block, [SELF])
        corner = join([sent(own, steps) for steps in corners])
        column = [sent(own, steps) for steps in above]
        (longest, corner, *column), _ = tied([column[0], corner, *column[1:]])
        near = join([own, longest, *column])
        (near, corner), _ = tied([near, corner])
        far = [sent(corner, steps) for steps in above]
        sides = [sent(near, steps) for steps in columns + lines]

        state = fold(layout, queries, None, [near, corner], groups)
        sides, state = tied(sides, state)
        others = swapped(sides) + swapped([join([corner, near])])
        state = fold(layout, queries, state, sides, groups)
        far, state = tied(far, state)
        far = [join(far)]
        far_others = swapped(far)
        state = fold(layout, queries, state, others, groups)
        return fold(layout, queries, state, far + far_others, groups, last=True)

    placed = P(AXES, None)
    return jax.shard_map(
        per_device, mesh=mesh, in_specs=(placed, placed, placed), out_specs=placed, check_vma=False
    )
```

```python
import functools
import math

import jax
import jax.numpy as jnp
from jax import lax
from jax.experimental import pallas as pl
from jax.experimental.pallas import tpu as pltpu
from jax.sharding import PartitionSpec as P

HD = 128
AXES = ("ctx", "kvh")
CORES = 2
HIDDEN = -1e30
HERE = (0, 0)
SELF = (HERE, 0, 0, 0)


class Layout:
    def __init__(self, mesh_shape):
        ctx, self.across = mesh_shape["ctx"], mesh_shape["kvh"]
        self.lines = 2
        self.planes = ctx // (CORES * self.lines)
        self.size = ctx * self.across

    def split(self, rank):
        column = rank % self.across
        core = rank // self.across % CORES
        line = rank // (self.across * CORES) % self.lines
        plane = rank // (self.across * CORES * self.lines)
        return plane, line, core, column

    def join(self, plane, line, core, column):
        return ((plane * self.lines + line) * CORES + core) * self.across + column

    def partner(self, rank, steps):
        (even, odd), line, swap, column = steps
        place = self.split(rank)
        up = even * (1 - place[2]) + odd * place[2]
        return self.join(place[0] ^ up, place[1] ^ line, place[2] ^ swap, place[3] ^ column)

    def exchange(self, array, steps):
        return lax.ppermute(array, AXES, [(rank, self.partner(rank, steps)) for rank in range(self.size)])

    def here(self):
        return lax.axis_index("ctx") * self.across + lax.axis_index("kvh")


def fold_kernel(layout, sources, rows, groups, carried, last, *refs):
    plane = layout.split(layout.here())[0]

    def run(ups):
        fold_blocks(layout, sources, rows, groups, carried, last, ups, *refs)

    every = {up for piece in sources for steps in piece for up in steps[0]}
    if every == {0}:
        run(every)
        return
    few = min(3, layout.planes - 1)
    for at in range(few):
        pl.when(plane == at)(functools.partial(run, {up for up in every if at ^ up <= at}))
    pl.when(plane >= few)(lambda: run(every))


def fold_blocks(layout, sources, rows, groups, carried, last, ups, *refs):
    refs = list(refs)
    query_ref = refs.pop(0)
    state_refs = [refs.pop(0) for _ in range(3)] if carried else None
    piece_refs, refs = refs[: len(sources)], refs[len(sources) :]
    out_refs, (score_ref, weight_ref) = refs[:-2], refs[-2:]
    blocks, runs = [], []
    for ref, piece in zip(piece_refs, sources, strict=True):
        for at, steps in enumerate(piece):
            if not ups.issuperset(steps[0]):
                continue
            blocks.append(steps)
            if runs and runs[-1][0] is ref and runs[-1][2] == at * rows:
                runs[-1][2] += rows
            else:
                runs.append([ref, at * rows, (at + 1) * rows])
    width = len(blocks) * rows
    heads = query_ref.shape[1] // (groups * HD)
    tall = heads * rows
    scale = math.log2(math.e) / math.sqrt(HD)

    rank = layout.here()
    along = lax.broadcasted_iota(jnp.int32, (1, width), 1)
    bias = jnp.zeros((1, width), jnp.float32)
    for at, steps in enumerate(blocks):
        hidden = layout.partner(rank, steps) > rank
        bias = jnp.where(along // rows == at, jnp.where(hidden, HIDDEN, 0.0).astype(jnp.float32), bias)
    own = blocks.index(SELF) * rows if SELF in blocks else None
    if own is not None:
        token = lax.broadcasted_iota(jnp.int32, (rows, width), 0)
        place = lax.broadcasted_iota(jnp.int32, (rows, width), 1) - own
        later = jnp.logical_and(place < rows, place > token)
        bias = jnp.where(jnp.logical_and(place >= 0, later), HIDDEN, bias)

    def write(group, largest, totals, summed):
        if last:
            first = group * heads * HD
            result = (summed / totals).astype(jnp.bfloat16)
            for h in range(heads):
                out_refs[0][:, first + h * HD : first + (h + 1) * HD] = result[h * rows : (h + 1) * rows]
        else:
            for ref, array in zip(out_refs, (largest, totals, summed), strict=True):
                ref[group] = array

    if not blocks:
        for group in range(groups):
            write(group, *(ref[group] for ref in state_refs))
        return

    def score(group):
        first = group * heads * HD
        query = jnp.concatenate([query_ref[:, first + h * HD : first + (h + 1) * HD] for h in range(heads)], axis=0)
        at = group * HD
        key = jnp.concatenate([ref[begin:end, at : at + HD] for ref, begin, end in runs], axis=0)
        score_ref[group % 2, :, :width] = lax.dot_general(
            query, key, (((1,), (1,)), ((), ())), preferred_element_type=jnp.float32
        )

    def mix(group):
        slot = group % 2
        tops, sums = [], []
        for begin in range(0, tall, rows):
            scores = score_ref[slot, begin : begin + rows, :width] * scale + bias
            top = jnp.broadcast_to(jnp.max(scores, axis=1, keepdims=True), (rows, HD))
            if carried:
                top = jnp.maximum(top, state_refs[0][group, begin : begin + rows])
            total = jnp.zeros((rows, HD), jnp.float32)
            rest = jnp.zeros((rows, 1), jnp.float32)
            for left in range(0, width, HD):
                part = min(HD, width - left)
                weights = jnp.exp2(scores[:, left : left + part] - top[:, :part])
                if part == HD:
                    total = total + weights
                else:
                    rest = jnp.sum(weights, axis=1, keepdims=True)
                weight_ref[slot, begin : begin + rows, left : left + part] = weights.astype(jnp.bfloat16)
            tops.append(top)
            sums.append(jnp.broadcast_to(jnp.sum(total, axis=1, keepdims=True) + rest, (rows, HD)))
        largest, totals = jnp.concatenate(tops, axis=0), jnp.concatenate(sums, axis=0)
        at = (groups + group) * HD
        value = jnp.concatenate([ref[begin:end, at : at + HD] for ref, begin, end in runs], axis=0)
        summed = jnp.dot(weight_ref[slot, :, :width], value, preferred_element_type=jnp.float32)
        if carried:
            decay = jnp.exp2(state_refs[0][group] - largest)
            totals = totals + state_refs[1][group] * decay
            summed = summed + state_refs[2][group] * decay
        write(group, largest, totals, summed)

    for begin in range(0, groups, 2):
        both = range(begin, min(begin + 2, groups))
        for group in both:
            score(group)
        for group in both:
            mix(group)


def fold(layout, queries, state, pieces, groups, last=False):
    rows, query_width = queries.shape
    tall = rows * query_width // (groups * HD)
    arrays = [array for array, _ in pieces]
    tokens = -(-sum(array.shape[0] for array in arrays) // HD) * HD
    carried = state is not None
    state_type = jax.ShapeDtypeStruct((groups, tall, HD), jnp.float32)
    whole = pl.BlockSpec(memory_space=pltpu.VMEM)
    return pl.pallas_call(
        functools.partial(
            fold_kernel, layout, [blocks for _, blocks in pieces], rows, groups, carried, last
        ),
        in_specs=[whole] * (1 + 3 * carried + len(arrays)),
        out_specs=whole if last else [whole] * 3,
        out_shape=jax.ShapeDtypeStruct(queries.shape, jnp.bfloat16) if last else [state_type] * 3,
        scratch_shapes=[pltpu.VMEM((2, tall, tokens), jnp.float32), pltpu.VMEM((2, tall, tokens), jnp.bfloat16)],
        compiler_params=pltpu.CompilerParams(vmem_limit_bytes=24 * 1024 * 1024),
        cost_estimate=pl.CostEstimate(flops=0, bytes_accessed=0, transcendentals=0),
    )(queries, *(state or ()), *arrays)


def solution(mesh):
    layout = Layout(dict(mesh.shape))

    def per_device(queries, keys, values):
        groups = keys.shape[1] // HD
        go = layout.exchange
        block = jnp.concatenate([keys, values], axis=1)
        above = [((up, up), 0, 0, 0) for up in range(layout.planes - 1, 0, -1)]
        columns = [(HERE, 0, 0, c) for c in range(1, layout.across)]
        lines = [(HERE, l, 0, 0) for l in range(1, layout.lines)]
        corners = [(HERE, l, 0, c) for _, l, _, _ in lines for _, _, _, c in columns]

        def moved(steps, by):
            def add(one):
                up = (one[0][0] ^ by[0][0], one[0][1] ^ by[0][1])
                return up, one[1] ^ by[1], one[2] ^ by[2], one[3] ^ by[3]

            return [add(one) for one in steps]

        def sent(piece, by):
            return go(piece[0], by), moved(piece[1], by)

        def swapped(pieces):
            turned = [sent(piece, (HERE, 0, 1, 0)) for piece in pieces]
            return [(array, [(up[::-1], l, swap, c) for up, l, swap, c in steps]) for array, steps in turned]

        def join(pieces):
            if len(pieces) == 1:
                return pieces[0]
            return jnp.concatenate([x for x, _ in pieces], axis=0), [one for _, steps in pieces for one in steps]

        def tied(pieces, state=None):
            arrays, state = lax.optimization_barrier(([array for array, _ in pieces], state))
            return [(array, steps) for array, (_, steps) in zip(arrays, pieces, strict=True)], state

        own = (block, [SELF])
        corner = join([sent(own, steps) for steps in corners])
        column = [sent(own, steps) for steps in above]
        (longest, corner, *column), _ = tied([column[0], corner, *column[1:]])
        near = join([own, longest, *column])
        (near, corner), _ = tied([near, corner])
        far = [sent(corner, steps) for steps in [above[0], *above[:0:-1]]]
        sides = [sent(near, steps) for steps in columns + lines]

        state = fold(layout, queries, None, [near, corner], groups)
        sides, state = tied(sides, state)
        others = swapped(sides) + swapped([join([corner, near])])
        state = fold(layout, queries, state, sides, groups)
        far, state = tied(far, state)
        far = [join(far)]
        far_others = swapped(far)
        state = fold(layout, queries, state, others, groups)
        return fold(layout, queries, state, far + far_others, groups, last=True)

    placed = P(AXES, None)
    return jax.shard_map(
        per_device, mesh=mesh, in_specs=(placed, placed, placed), out_specs=placed, check_vma=False
    )
```

```python
import functools
import math

import jax
import jax.numpy as jnp
from jax import lax
from jax.experimental import pallas as pl
from jax.experimental.pallas import tpu as pltpu
from jax.sharding import PartitionSpec as P

HD = 128
AXES = ("ctx", "kvh")
CORES = 2
HIDDEN = -1e30
HERE = (0, 0)
SELF = (HERE, 0, 0, 0)


class Layout:
    def __init__(self, mesh_shape):
        ctx, self.across = mesh_shape["ctx"], mesh_shape["kvh"]
        self.lines = 2
        self.planes = ctx // (CORES * self.lines)
        self.size = ctx * self.across

    def split(self, rank):
        column = rank % self.across
        core = rank // self.across % CORES
        line = rank // (self.across * CORES) % self.lines
        plane = rank // (self.across * CORES * self.lines)
        return plane, line, core, column

    def join(self, plane, line, core, column):
        return ((plane * self.lines + line) * CORES + core) * self.across + column

    def partner(self, rank, steps):
        (even, odd), line, swap, column = steps
        place = self.split(rank)
        up = even * (1 - place[2]) + odd * place[2]
        return self.join(place[0] ^ up, place[1] ^ line, place[2] ^ swap, place[3] ^ column)

    def exchange(self, array, steps):
        return lax.ppermute(array, AXES, [(rank, self.partner(rank, steps)) for rank in range(self.size)])

    def here(self):
        return lax.axis_index("ctx") * self.across + lax.axis_index("kvh")


def fold_kernel(layout, sources, rows, groups, carried, last, *refs):
    plane = layout.split(layout.here())[0]

    def run(ups):
        fold_blocks(layout, sources, rows, groups, carried, last, ups, *refs)

    every = {up for piece in sources for steps in piece for up in steps[0]}
    if every == {0}:
        run(every)
        return
    few = min(3, layout.planes - 1)
    for at in range(few):
        pl.when(plane == at)(functools.partial(run, {up for up in every if at ^ up <= at}))
    pl.when(plane >= few)(lambda: run(every))


def fold_blocks(layout, sources, rows, groups, carried, last, ups, *refs):
    refs = list(refs)
    query_ref = refs.pop(0)
    state_refs = [refs.pop(0) for _ in range(3)] if carried else None
    piece_refs, refs = refs[: len(sources)], refs[len(sources) :]
    out_refs, (score_ref, weight_ref) = refs[:-2], refs[-2:]
    blocks, runs = [], []
    for ref, piece in zip(piece_refs, sources, strict=True):
        for at, steps in enumerate(piece):
            if not ups.issuperset(steps[0]):
                continue
            blocks.append(steps)
            if runs and runs[-1][0] is ref and runs[-1][2] == at * rows:
                runs[-1][2] += rows
            else:
                runs.append([ref, at * rows, (at + 1) * rows])
    width = len(blocks) * rows
    heads = query_ref.shape[1] // (groups * HD)
    tall = heads * rows
    scale = math.log2(math.e) / math.sqrt(HD)

    rank = layout.here()
    along = lax.broadcasted_iota(jnp.int32, (1, width), 1)
    bias = jnp.zeros((1, width), jnp.float32)
    for at, steps in enumerate(blocks):
        hidden = layout.partner(rank, steps) > rank
        bias = jnp.where(along // rows == at, jnp.where(hidden, HIDDEN, 0.0).astype(jnp.float32), bias)
    own = blocks.index(SELF) * rows if SELF in blocks else None
    if own is not None:
        token = lax.broadcasted_iota(jnp.int32, (rows, width), 0)
        place = lax.broadcasted_iota(jnp.int32, (rows, width), 1) - own
        later = jnp.logical_and(place < rows, place > token)
        bias = jnp.where(jnp.logical_and(place >= 0, later), HIDDEN, bias)

    def write(group, largest, totals, summed):
        if last:
            first = group * heads * HD
            result = (summed / totals).astype(jnp.bfloat16)
            for h in range(heads):
                out_refs[0][:, first + h * HD : first + (h + 1) * HD] = result[h * rows : (h + 1) * rows]
        else:
            for ref, array in zip(out_refs, (largest, totals, summed), strict=True):
                ref[group] = array

    if not blocks:
        for group in range(groups):
            write(group, *(ref[group] for ref in state_refs))
        return

    def score(group):
        first = group * heads * HD
        query = jnp.concatenate([query_ref[:, first + h * HD : first + (h + 1) * HD] for h in range(heads)], axis=0)
        at = group * HD
        key = jnp.concatenate([ref[begin:end, at : at + HD] for ref, begin, end in runs], axis=0)
        score_ref[group % 2, :, :width] = lax.dot_general(
            query, key, (((1,), (1,)), ((), ())), preferred_element_type=jnp.float32
        )

    def mix(group):
        slot = group % 2
        tops, sums = [], []
        for begin in range(0, tall, rows):
            scores = score_ref[slot, begin : begin + rows, :width] * scale + bias
            top = jnp.broadcast_to(jnp.max(scores, axis=1, keepdims=True), (rows, HD))
            if carried:
                top = jnp.maximum(top, state_refs[0][group, begin : begin + rows])
            total = jnp.zeros((rows, HD), jnp.float32)
            rest = jnp.zeros((rows, 1), jnp.float32)
            for left in range(0, width, HD):
                part = min(HD, width - left)
                weights = jnp.exp2(scores[:, left : left + part] - top[:, :part])
                if part == HD:
                    total = total + weights
                else:
                    rest = jnp.sum(weights, axis=1, keepdims=True)
                weight_ref[slot, begin : begin + rows, left : left + part] = weights.astype(jnp.bfloat16)
            tops.append(top)
            sums.append(jnp.broadcast_to(jnp.sum(total, axis=1, keepdims=True) + rest, (rows, HD)))
        largest, totals = jnp.concatenate(tops, axis=0), jnp.concatenate(sums, axis=0)
        at = (groups + group) * HD
        value = jnp.concatenate([ref[begin:end, at : at + HD] for ref, begin, end in runs], axis=0)
        summed = jnp.dot(weight_ref[slot, :, :width], value, preferred_element_type=jnp.float32)
        if carried:
            decay = jnp.exp2(state_refs[0][group] - largest)
            totals = totals + state_refs[1][group] * decay
            summed = summed + state_refs[2][group] * decay
        write(group, largest, totals, summed)

    for begin in range(0, groups, 2):
        both = range(begin, min(begin + 2, groups))
        for group in both:
            score(group)
        for group in both:
            mix(group)


def fold(layout, queries, state, pieces, groups, last=False):
    rows, query_width = queries.shape
    tall = rows * query_width // (groups * HD)
    arrays = [array for array, _ in pieces]
    tokens = -(-sum(array.shape[0] for array in arrays) // HD) * HD
    carried = state is not None
    state_type = jax.ShapeDtypeStruct((groups, tall, HD), jnp.float32)
    whole = pl.BlockSpec(memory_space=pltpu.VMEM)
    return pl.pallas_call(
        functools.partial(
            fold_kernel, layout, [blocks for _, blocks in pieces], rows, groups, carried, last
        ),
        in_specs=[whole] * (1 + 3 * carried + len(arrays)),
        out_specs=whole if last else [whole] * 3,
        out_shape=jax.ShapeDtypeStruct(queries.shape, jnp.bfloat16) if last else [state_type] * 3,
        scratch_shapes=[pltpu.VMEM((2, tall, tokens), jnp.float32), pltpu.VMEM((2, tall, tokens), jnp.bfloat16)],
        compiler_params=pltpu.CompilerParams(vmem_limit_bytes=24 * 1024 * 1024),
        cost_estimate=pl.CostEstimate(flops=0, bytes_accessed=0, transcendentals=0),
    )(queries, *(state or ()), *arrays)


def solution(mesh):
    layout = Layout(dict(mesh.shape))

    def per_device(queries, keys, values):
        groups = keys.shape[1] // HD
        go = layout.exchange
        block = jnp.concatenate([keys, values], axis=1)
        above = [((up, up), 0, 0, 0) for up in range(layout.planes - 1, 0, -1)]
        columns = [(HERE, 0, 0, c) for c in range(1, layout.across)]
        lines = [(HERE, l, 0, 0) for l in range(1, layout.lines)]
        corners = [(HERE, l, 0, c) for _, l, _, _ in lines for _, _, _, c in columns]

        def moved(steps, by):
            def add(one):
                up = (one[0][0] ^ by[0][0], one[0][1] ^ by[0][1])
                return up, one[1] ^ by[1], one[2] ^ by[2], one[3] ^ by[3]

            return [add(one) for one in steps]

        def sent(piece, by):
            return go(piece[0], by), moved(piece[1], by)

        def swapped(pieces):
            turned = [sent(piece, (HERE, 0, 1, 0)) for piece in pieces]
            return [(array, [(up[::-1], l, swap, c) for up, l, swap, c in steps]) for array, steps in turned]

        def join(pieces):
            if len(pieces) == 1:
                return pieces[0]
            return jnp.concatenate([x for x, _ in pieces], axis=0), [one for _, steps in pieces for one in steps]

        def tied(pieces, state=None):
            arrays, state = lax.optimization_barrier(([array for array, _ in pieces], state))
            return [(array, steps) for array, (_, steps) in zip(arrays, pieces, strict=True)], state

        own = (block, [SELF])
        corner = join([sent(own, steps) for steps in corners])
        column = [sent(own, steps) for steps in above]
        (longest, corner, *column), _ = tied([column[0], corner, *column[1:]])
        near = join([own, longest, *column])
        (near, corner), _ = tied([near, corner])
        far = [sent(corner, steps) for steps in [above[0], *above[:0:-1]]]
        sides = [sent(near, steps) for steps in columns + lines]

        state = fold(layout, queries, None, [near, corner], groups)
        sides, state = tied(sides, state)
        others = swapped([join([corner, near])]) + swapped(sides)
        state = fold(layout, queries, state, sides, groups)
        far, state = tied(far, state)
        far = [join(far)]
        far_others = swapped(far)
        state = fold(layout, queries, state, others, groups)
        return fold(layout, queries, state, far + far_others, groups, last=True)

    placed = P(AXES, None)
    return jax.shard_map(
        per_device, mesh=mesh, in_specs=(placed, placed, placed), out_specs=placed, check_vma=False
    )
```
